32 devices in a mesh: groups: 2 (over x), tile: 16 (over z, y, core).
Axes of the slice: x: 2, y: 2, z: 4, core: 2. Of those that a mesh axis runs over, the one named last changes fastest.
Arguments:
- tiles: float32 [2, 12288, 384], P(None, ('groups', 'tile')), parts along dimension 1, may hold values from -6 to 6
- library: float32 [128, 2, 128, 128], P('tile'), may hold values from -6 to 6
- block_owner: int32 [2], replicated, may hold values from 0 to 15
- block_clips: int32 [2, 2], replicated, may hold values from 0 to 7
- layer_order: int32 [32, 2], P(('groups', 'tile')), parts along dimension 0, may hold values from 0 to 1, each once within a row
Outputs:
- scores: float32 [2, 2, 12288, 384], P(None, None, ('groups', 'tile')), parts along dimension 2
- peak_scores: float32 [4, 2], P('groups'), parts along dimension 0
The draws below stay inside these ranges and needn't reach their ends.
There are 2 independent parts, one for each index of `groups`. The reference program is written for one: setup_inputs(seed, part) draws one part's arguments, and reference() takes and returns one part's arrays. A program takes and returns all parts, laid end to end along the dimension named above; an argument that names none is the same for every part. Nothing has to cross between parts.
Inputs may be any that keep to these rules, and one draw needn't show every extreme that they name: `layer_order`: each row is a permutation of 0 to 1.
All inputs are finite; a program needn't handle non-finite values.
Results may differ from the reference program's by a relative error of at most 0.000098.
Values sent between devices are 32-bit elements; how exact they have to be, the bound alone decides.
No kernel may reach another device: no remote copies, remote signals or barrier semaphores. Data moves between devices by JAX's collectives and lax.ppermute only.
A program may use at most 128 MiB of HBM per device.

```python
import math
import jax
import jax.numpy as jnp
from jax import lax

SPAN = 512
CLIP = 128
LAYERS = 2
CLIPS_DEV = 8
BLOCKS = 2
PER_BLOCK = 2
ROWS = 384
COLS = 384
TILES = 16
LIBRARY = 128


def place_ends(drawn, rng, low, top_value):
    place = [jax.random.randint(jax.random.fold_in(rng, axis), (), 0, length) for axis, length in enumerate(drawn.shape)]
    main_axis = drawn.shape.index(max(drawn.shape))
    neighbour = place[:main_axis] + [(place[main_axis] + 1) % drawn.shape[main_axis]] + place[main_axis + 1:]
    return drawn.at[tuple(place)].set(low).at[tuple(neighbour)].set(top_value)


def levels(key, shape, pieces, least, top_value):
    gain, own = 1.0, jax.random.fold_in(key, 6)
    for axis_at, parts in pieces:
        steps = jnp.exp(jax.random.uniform(jax.random.fold_in(own, axis_at), (parts,), jnp.float32, least / len(pieces), top_value / len(pieces)))
        gain = gain * jnp.repeat(steps, shape[axis_at] // parts).reshape([-1 if axis == axis_at else 1 for axis in range(len(shape))])
    return gain


def centred(stream_key, shape, width, most, split=(), held_as=jnp.bfloat16):
    drawn = width * jax.random.normal(stream_key, shape, jnp.float32)
    if split:
        drawn = drawn * levels(stream_key, shape, split, -0.22, 0.18)
    return jnp.clip(drawn, -most, most).astype(held_as)


def setup_inputs(seed: int = 0, part: int = 0) -> dict:
    seeds = jax.random.split(jax.random.key(seed), 6)
    own_keys = jax.random.split(jax.random.fold_in(seeds[5], part), 6)
    return {
        "tiles": centred(own_keys[0], (LAYERS, TILES * ROWS, COLS), 1.0, 6.0, ((1, 16),), jnp.float32),
        "library": centred(seeds[1], (LIBRARY, LAYERS, CLIP, CLIP), 1.0, 6.0, ((0, 16),), jnp.float32),
        "block_owner": jax.random.randint(seeds[2], (BLOCKS,), 0, TILES).astype(jnp.int32),
        "block_clips": place_ends(jax.random.randint(seeds[3], (BLOCKS, PER_BLOCK), 0, CLIPS_DEV), jax.random.fold_in(seeds[3], 1), 0, CLIPS_DEV - 1).astype(jnp.int32),
        "layer_order": jax.vmap(lambda own: jax.random.permutation(own, LAYERS))(jax.random.split(own_keys[4], TILES)).reshape((TILES, LAYERS)).astype(jnp.int32),
    }


def window_band(length, starts, extent, number_type):
    position = jnp.arange(length)[:, None]
    anchor = jnp.arange(starts)[None, :]
    offset = position - anchor
    return ((offset >= 0) & (offset < extent)).astype(number_type)

def reference(tiles, library, block_owner, block_clips, layer_order):
    chosen = (block_owner[:, None] * CLIPS_DEV + block_clips).reshape(-1).astype(jnp.int32)
    chosen_clips = library[chosen]
    clip_rms = jnp.sqrt(lax.optimization_barrier(jnp.mean(chosen_clips * chosen_clips, axis=(1, 2, 3))) + 1e-05)
    padded_clips = jnp.pad(chosen_clips, ((0, 0), (0, 0), (0, SPAN - CLIP), (0, SPAN - CLIP)))
    clip_spectra = jnp.conj(jnp.fft.fft2(padded_clips))
    strip_rows = tiles.reshape(LAYERS, TILES, ROWS, COLS)
    following = jnp.concatenate([strip_rows[:, 1:, :CLIP, :], jnp.zeros((LAYERS, 1, CLIP, COLS), tiles.dtype)], axis=1)
    extended = jnp.moveaxis(jnp.concatenate([strip_rows, following], axis=2), 1, 0)
    band_rows = window_band(SPAN, ROWS, CLIP, tiles.dtype)
    band_cols = window_band(COLS, COLS, CLIP, tiles.dtype)
    root_count = math.sqrt(LAYERS * CLIP * CLIP)

    def one_tile(inputs):
        tile_block, layer_pick = inputs
        padded = jnp.pad(tile_block, ((0, 0), (0, 0), (0, SPAN - COLS)))
        spectra = jnp.fft.fft2(padded)
        crossed = lax.optimization_barrier(jnp.sum(spectra[None] * clip_spectra[:, layer_pick], axis=1))
        correlation = jnp.real(jnp.fft.ifft2(crossed))[:, :ROWS, :COLS]
        squares = lax.optimization_barrier(jnp.sum(tile_block * tile_block, axis=0))
        energy = jnp.dot(jnp.dot(band_rows.T, squares, precision=lax.Precision.HIGHEST), band_cols, precision=lax.Precision.HIGHEST)
        window_rms = jnp.sqrt(energy / (LAYERS * CLIP * CLIP) + 1e-05)
        return correlation / (root_count * clip_rms[:, None, None] * window_rms[None])
    all_scores = lax.map(one_tile, (extended, layer_order))
    all_scores = jnp.moveaxis(all_scores, 1, 0).reshape(BLOCKS, PER_BLOCK, TILES * ROWS, COLS)
    peak_scores = lax.optimization_barrier(jnp.max(all_scores, axis=(2, 3)))
    return (all_scores, peak_scores)
```

```python
import math

import jax
import jax.numpy as jnp
import ml_dtypes
import numpy as np
from jax import lax
from jax.experimental import pallas as pl
from jax.experimental.pallas import tpu as pltpu
from jax.sharding import PartitionSpec as P

SIGNS = (math.sqrt(2.0), -math.sqrt(2.0))


def halves(matrix):
    high = matrix.astype(ml_dtypes.bfloat16)
    low = (matrix - high.astype(np.float64)).astype(ml_dtypes.bfloat16)
    return high, low


def evaluation(e, ring):
    k = np.arange(2 * e)
    k = k[np.isin(k % 4, (0, 3) if ring == 0 else (1, 2))]
    angles = np.outer(2 * k + 1, np.arange(2 * e)) % (8 * e) * (2.0 * np.pi / (8 * e))
    return np.concatenate([np.cos(angles), np.sin(angles)], axis=0)


def left_factor(matrix):
    high, low = halves(matrix)
    return np.concatenate([high, low, high], axis=1)


def right_factor(matrix):
    high, low = halves(matrix)
    return np.concatenate([high, low, high], axis=0)


def factors(e):
    ev = [evaluation(e, ring) for ring in range(2)]
    inv = [np.linalg.inv(m) / (4.0 * math.sqrt(2.0)) for m in ev]
    inv_cols = [np.linalg.inv(m) / (2.0 * math.sqrt(2.0)) for m in ev]
    tile_left = np.stack([left_factor(m) for m in ev])
    tile_right = np.stack([right_factor(m.T) for m in ev])
    clip_left = left_factor(np.concatenate([m[:, :e] for m in ev], axis=0))
    clip_right = right_factor(np.concatenate([m[:, :e].T for m in ev], axis=1))
    back_left = np.stack([left_factor(m) for m in inv])
    back_right = np.stack([right_factor(m.T) for m in inv_cols])
    return tile_left, tile_right, clip_left, clip_right, back_left, back_right


def bands(e):
    position = np.arange(2 * e)[None, :] - np.arange(e)[:, None]
    band = ((position >= 0) & (position < e)).astype(ml_dtypes.bfloat16)
    return np.concatenate([band, band], axis=1), np.concatenate([band.T, band.T], axis=0)


def split(values):
    high = values.astype(jnp.bfloat16)
    return high, (values - high.astype(jnp.float32)).astype(jnp.bfloat16)


def dot(a, b):
    return jnp.dot(a, b, preferred_element_type=jnp.float32)


def beside(values):
    high, low = split(values)
    return jnp.concatenate([high, high, low], axis=1)


def stacked(values):
    high, low = split(values)
    return jnp.concatenate([high, high, low], axis=0)


def tile_kernel(tile, halo, left, right, band_rows, band_cols, spectrum, inverse_rms):
    layers, rows, columns = tile.shape
    e = halo.shape[1]
    blocks = [[tile[l, b * e : (b + 1) * e, :] for b in range(3)] + [halo[l]] for l in range(layers)]
    for l in range(layers):
        a0, a1, a2, a3 = blocks[l]
        for si, s in enumerate(SIGNS):
            folded = jnp.concatenate([a0 - a2 - s * a3, a1 + s * a2 + a3], axis=0)
            c0, c1, c2 = (folded[:, b * e : (b + 1) * e] for b in range(3))
            along = []
            for ti, t in enumerate(SIGNS):
                ring = jnp.concatenate([c0 - c2, c1 + t * c2], axis=1)
                along.append(dot(beside(ring), right[ti]))
            both = dot(left[si], stacked(jnp.concatenate(along, axis=1)))
            for ti in range(2):
                at = ti * 2 * e
                cc, cs = both[:e, at : at + e], both[:e, at + e : at + 2 * e]
                sc, ss = both[e:, at : at + e], both[e:, at + e : at + 2 * e]
                lanes = slice(ti * e, (ti + 1) * e)
                place = slice(si * e, (si + 1) * e)
                spectrum[l, 0, place, lanes] = cc - ss
                spectrum[l, 1, place, lanes] = -(cs + sc)
                spectrum[l, 2, place, lanes] = cc + ss
                spectrum[l, 3, place, lanes] = sc - cs
    squares = [sum(blocks[l][b] * blocks[l][b] for l in range(layers)) for b in range(4)]
    parts = [split(v) for v in squares]
    for b in range(3):
        tall = jnp.concatenate([parts[b][0], parts[b + 1][0], parts[b][1], parts[b + 1][1]], axis=0)
        summed = dot(band_rows[...], tall)
        high, low = split(summed)
        for c in range(3):
            pair = (high[:, c * e : (c + 2) * e], low[:, c * e : (c + 2) * e])
            if c < 2:
                energy = dot(jnp.concatenate(pair, axis=1), band_cols[...])
            else:
                energy = dot(pair[0], band_cols[:e, :]) + dot(pair[1], band_cols[:e, :])
            inverse_rms[b * e : (b + 1) * e, c * e : (c + 1) * e] = lax.rsqrt(
                energy * (1.0 / (layers * e * e)) + 1e-05
            )


def score_kernel(
    slots, order, clip, spectrum, inverse_rms, clip_left, clip_right, back_left, back_right, *rest
):
    scores, peaks = rest[-2:]
    layers, e, _ = clip.shape
    root = math.sqrt(layers * e * e)
    first = [clip[order[l]] for l in range(layers)]
    total = sum(jnp.sum(v * v, keepdims=True) for v in first)
    scale = lax.rsqrt(total * (1.0 / (layers * e * e)) + 1e-05) * (1.0 / root)
    along = dot(beside(jnp.concatenate(first, axis=0)), clip_right[...])
    both = [dot(clip_left[...], stacked(along[l * e : (l + 1) * e])) for l in range(layers)]
    rows = []
    for si in range(2):
        upper, lower = [], []
        for ti in range(2):
            at, up = ti * 2 * e, si * 2 * e
            rp = ip = rm = im = 0.0
            for l in range(layers):
                cc, cs = both[l][up : up + e, at : at + e], both[l][up : up + e, at + e : at + 2 * e]
                sc = both[l][up + e : up + 2 * e, at : at + e]
                ss = both[l][up + e : up + 2 * e, at + e : at + 2 * e]
                xpr, xpi, xmr, xmi = (
                    spectrum[l, j, si * e : (si + 1) * e, ti * e : (ti + 1) * e] for j in range(4)
                )
                kpr, kpi, kmr, kmi = cc - ss, cs + sc, cc + ss, sc - cs
                rp = rp + (xpr * kpr - xpi * kpi)
                ip = ip + (xpi * kpr + xpr * kpi)
                rm = rm + (xmr * kmr + xmi * kmi)
                im = im + (xmi * kmr - xmr * kmi)
            upper += [rp + rm, -(ip + im)]
            lower += [im - ip, rm - rp]
        rows.append(
            jnp.concatenate([jnp.concatenate(upper, axis=1), jnp.concatenate(lower, axis=1)], axis=0)
        )
    p, m = (dot(back_left[si], stacked(rows[si])) for si in range(2))
    b2 = p[e:] - m[e:]
    b0 = SIGNS[0] * (p[:e] + m[:e]) + b2
    b1 = SIGNS[0] * (p[e:] + m[e:]) + (p[:e] - m[:e])
    back = jnp.concatenate([b0, b1, b2], axis=0)
    p, m = (
        dot(beside(back[:, ti * 2 * e : (ti + 1) * 2 * e]), back_right[ti]) for ti in range(2)
    )
    b2 = p[:, e:] - m[:, e:]
    b0 = SIGNS[0] * (p[:, :e] + m[:, :e]) + b2
    b1 = SIGNS[0] * (p[:, e:] + m[:, e:]) + (p[:, :e] - m[:, :e])
    result = jnp.concatenate([b0, b1, b2], axis=1) * inverse_rms[...] * scale
    scores[...] = result
    largest = jnp.max(result)
    i = pl.program_id(0)

    @pl.when(i == 0)
    def _():
        peaks[...] = jnp.full(peaks.shape, -jnp.inf, jnp.float32)

    row = lax.broadcasted_iota(jnp.int32, peaks.shape, 0)
    peaks[...] = jnp.where(row == slots[i], largest, peaks[...])


def whole(array):
    return pl.BlockSpec(array.shape, lambda *_: (0,) * array.ndim)


def tile_call(tiles, halo, consts):
    layers, rows, columns = tiles.shape
    e = halo.shape[1]
    args = (tiles, halo) + consts
    return pl.pallas_call(
        tile_kernel,
        out_shape=(
            jax.ShapeDtypeStruct((layers, 4, 2 * e, 2 * e), jnp.float32),
            jax.ShapeDtypeStruct((rows, columns), jnp.float32),
        ),
        compiler_params=pltpu.CompilerParams(vmem_limit_bytes=48 * 1024 * 1024),
        cost_estimate=pl.CostEstimate(flops=2_000_000_000, bytes_accessed=6_000_000, transcendentals=0),
    )(*args)


def score_call(slots, order, clips, spectrum, inverse_rms, consts, count, before):
    n, layers, e, _ = clips.shape
    rows, columns = inverse_rms.shape
    fixed = (spectrum, inverse_rms) + consts
    in_specs = [pl.BlockSpec((None, layers, e, e), lambda i, *_: (i, 0, 0, 0))]
    in_specs += [whole(a) for a in fixed]
    args = (clips,) + fixed
    aliases = {}
    if before is not None:
        in_specs.append(pl.BlockSpec(memory_space=pl.ANY))
        args += (before,)
        aliases = {2 + len(args) - 1: 0}
    return pl.pallas_call(
        score_kernel,
        grid_spec=pltpu.PrefetchScalarGridSpec(
            num_scalar_prefetch=2,
            grid=(n,),
            in_specs=in_specs,
            out_specs=(
                pl.BlockSpec((None, rows, columns), lambda i, slots, order: (slots[i], 0, 0)),
                pl.BlockSpec((8, 128), lambda i, *_: (0, 0)),
            ),
        ),
        out_shape=(
            jax.ShapeDtypeStruct((count, rows, columns), jnp.float32),
            jax.ShapeDtypeStruct((8, 128), jnp.float32),
        ),
        input_output_aliases=aliases,
        compiler_params=pltpu.CompilerParams(
            vmem_limit_bytes=56 * 1024 * 1024, dimension_semantics=("arbitrary",)
        ),
        cost_estimate=pl.CostEstimate(
            flops=n * 1_300_000_000, bytes_accessed=6_000_000, transcendentals=0
        ),
    )(slots, order, *args)


def swap(block, axis, distance):
    return lax.ppermute(block, axis, [(i, i ^ distance) for i in range(lax.axis_size(axis))])


def local(tiles, library, block_owner, block_clips, layer_order):
    layers, rows, columns = tiles.shape
    e = library.shape[-1]
    assert rows == 3 * e and columns == 3 * e and layers * e <= 256
    blocks, per_block = block_clips.shape
    devices = lax.axis_size("tile")
    assert blocks == 2 and per_block == 2 and devices & (devices - 1) == 0
    tile_left, tile_right, clip_left, clip_right, back_left, back_right = map(jnp.asarray, factors(e))
    band_rows, band_cols = map(jnp.asarray, bands(e))

    me = lax.axis_index("tile")
    core = me % 2
    block = lax.axis_index("groups") % 2
    owner = block_owner[block]
    chosen = lax.dynamic_index_in_dim(block_clips, block, 0, keepdims=False)
    mine = lax.dynamic_index_in_dim(library, chosen[core], 0, keepdims=False)
    theirs = lax.dynamic_index_in_dim(library, chosen[1 - core], 0, keepdims=False)
    differ = owner ^ me
    got = swap(theirs, "tile", 1)
    held = jnp.where((differ & 1) == 0, mine, got)
    distance = 2
    while distance < devices:
        got = swap(held, "tile", distance)
        held = jnp.where((differ & distance) == 0, held, got)
        distance *= 2
    other = swap(held, "groups", 1)
    rest = swap(jnp.stack([held, other]), "tile", 1)
    later = jnp.concatenate([other[None], rest], axis=0)

    route = [(i, i - 1) for i in range(1, devices)]
    halo = lax.ppermute(tiles[:, :e, :], "tile", route)
    spectrum, inverse_rms = tile_call(
        tiles, halo, (tile_left, tile_right, band_rows, band_cols)
    )
    consts = (clip_left, clip_right, back_left, back_right)
    order = layer_order[0]
    count = blocks * per_block
    slot = block * per_block + core
    first = slot[None].astype(jnp.int32)
    second = jnp.stack([slot ^ 2, slot ^ 1, slot ^ 3]).astype(jnp.int32)
    scores, peaks = score_call(first, order, held[None], spectrum, inverse_rms, consts, count, None)
    scores, more = score_call(second, order, later, spectrum, inverse_rms, consts, count, scores)
    best = jnp.maximum(peaks, more)
    distance = 1
    while distance < devices:
        best = jnp.maximum(best, swap(best, "tile", distance))
        distance *= 2
    return (
        scores.reshape(blocks, per_block, rows, columns),
        best[:count, 0].reshape(blocks, per_block),
    )


def solution(mesh):
    in_specs = (
        P(None, ("groups", "tile"), None),
        P("tile", None, None, None),
        P(),
        P(),
        P(("groups", "tile"), None),
    )
    out_specs = (P(None, None, ("groups", "tile"), None), P("groups", None))
    return jax.shard_map(local, mesh=mesh, in_specs=in_specs, out_specs=out_specs, check_vma=False)
```

```python
import math

import jax
import jax.numpy as jnp
import ml_dtypes
import numpy as np
from jax import lax
from jax.experimental import pallas as pl
from jax.experimental.pallas import tpu as pltpu
from jax.sharding import PartitionSpec as P

SIGNS = (math.sqrt(2.0), -math.sqrt(2.0))
VMEM = 20 * 1024 * 1024
MOST = 40 * 1024 * 1024
WHOLE = 57 * 1024 * 1024


def halves(matrix):
    high = matrix.astype(ml_dtypes.bfloat16)
    low = (matrix - high.astype(np.float64)).astype(ml_dtypes.bfloat16)
    return high, low


def evaluation(e, ring):
    k = np.arange(2 * e)
    k = k[np.isin(k % 4, (0, 3) if ring == 0 else (1, 2))]
    angles = np.outer(2 * k + 1, np.arange(2 * e)) % (8 * e) * (2.0 * np.pi / (8 * e))
    return np.concatenate([np.cos(angles), np.sin(angles)], axis=0)


def left_factor(matrix):
    high, low = halves(matrix)
    return np.concatenate([high, low, high], axis=1)


def right_factor(matrix):
    high, low = halves(matrix)
    return np.concatenate([high, low, high], axis=0)


def factors(e):
    ev = [evaluation(e, ring) for ring in range(2)]
    inv = [np.linalg.inv(m) / (4.0 * math.sqrt(2.0)) for m in ev]
    inv_cols = [np.linalg.inv(m) / (2.0 * math.sqrt(2.0)) for m in ev]
    tile_left = np.stack([left_factor(m) for m in ev])
    tile_right = np.stack([right_factor(m.T) for m in ev])
    clip_left = left_factor(np.concatenate([m[:, :e] for m in ev], axis=0))
    clip_right = right_factor(np.concatenate([m[:, :e].T for m in ev], axis=1))
    back_left = np.stack([left_factor(m) for m in inv])
    back_right = np.stack([right_factor(m.T) for m in inv_cols])
    return tile_left, tile_right, clip_left, clip_right, back_left, back_right


def bands(e):
    position = np.arange(2 * e)[None, :] - np.arange(e)[:, None]
    band = ((position >= 0) & (position < e)).astype(ml_dtypes.bfloat16)
    return np.concatenate([band, band], axis=1), np.concatenate([band.T, band.T], axis=0)


def split(values):
    high = values.astype(jnp.bfloat16)
    return high, (values - high.astype(jnp.float32)).astype(jnp.bfloat16)


def dot(a, b):
    return jnp.dot(a, b, preferred_element_type=jnp.float32)


def beside(values):
    high, low = split(values)
    return jnp.concatenate([high, high, low], axis=1)


def stacked(values):
    high, low = split(values)
    return jnp.concatenate([high, high, low], axis=0)


def tile_kernel(tile, halo, band_rows, band_cols, right, left, spectrum, inverse_rms):
    layers, rows, columns = tile.shape
    e = halo.shape[1]
    blocks = [[tile[l, b * e : (b + 1) * e, :] for b in range(3)] + [halo[l]] for l in range(layers)]
    squares = [sum(blocks[l][b] * blocks[l][b] for l in range(layers)) for b in range(4)]
    parts = [split(v) for v in squares]
    for b in range(3):
        tall = jnp.concatenate([parts[b][0], parts[b + 1][0], parts[b][1], parts[b + 1][1]], axis=0)
        summed = dot(band_rows[...], tall)
        high, low = split(summed)
        for c in range(3):
            pair = (high[:, c * e : (c + 2) * e], low[:, c * e : (c + 2) * e])
            if c < 2:
                energy = dot(jnp.concatenate(pair, axis=1), band_cols[...])
            else:
                energy = dot(pair[0], band_cols[:e, :]) + dot(pair[1], band_cols[:e, :])
            inverse_rms[b * e : (b + 1) * e, c * e : (c + 1) * e] = lax.rsqrt(
                energy * (1.0 / (layers * e * e)) + 1e-05
            )
    for l in range(layers):
        a0, a1, a2, a3 = blocks[l]
        for si, s in enumerate(SIGNS):
            folded = jnp.concatenate([a0 - a2 - s * a3, a1 + s * a2 + a3], axis=0)
            c0, c1, c2 = (folded[:, b * e : (b + 1) * e] for b in range(3))
            along = []
            for ti, t in enumerate(SIGNS):
                ring = jnp.concatenate([c0 - c2, c1 + t * c2], axis=1)
                along.append(dot(beside(ring), right[ti]))
            both = dot(left[si], stacked(jnp.concatenate(along, axis=1)))
            for ti in range(2):
                at = ti * 2 * e
                cc, cs = both[:e, at : at + e], both[:e, at + e : at + 2 * e]
                sc, ss = both[e:, at : at + e], both[e:, at + e : at + 2 * e]
                lanes = slice(ti * e, (ti + 1) * e)
                place = slice(si * e, (si + 1) * e)
                spectrum[l, 0, place, lanes] = cc - ss
                spectrum[l, 1, place, lanes] = -(cs + sc)
                spectrum[l, 2, place, lanes] = cc + ss
                spectrum[l, 3, place, lanes] = sc - cs


def score_clip(
    order, clip, spectrum, inverse_rms, clip_left, clip_right, back_left, back_right, scores
):
    layers, e, _ = clip.shape
    root = math.sqrt(layers * e * e)
    first = []
    for l in range(layers):
        matched = clip[0]
        for m in range(1, layers):
            matched = jnp.where(order[l : l + 1, :] == m, clip[m], matched)
        first.append(matched)
    total = sum(jnp.sum(v * v, keepdims=True) for v in first)
    scale = lax.rsqrt(total * (1.0 / (layers * e * e)) + 1e-05) * (1.0 / root)
    along = dot(beside(jnp.concatenate(first, axis=0)), clip_right[...])
    both = [dot(clip_left[...], stacked(along[l * e : (l + 1) * e])) for l in range(layers)]
    rows = []
    for si in range(2):
        upper, lower = [], []
        for ti in range(2):
            at, up = ti * 2 * e, si * 2 * e
            rp = ip = rm = im = 0.0
            for l in range(layers):
                cc, cs = both[l][up : up + e, at : at + e], both[l][up : up + e, at + e : at + 2 * e]
                sc = both[l][up + e : up + 2 * e, at : at + e]
                ss = both[l][up + e : up + 2 * e, at + e : at + 2 * e]
                xpr, xpi, xmr, xmi = (
                    spectrum[l, j, si * e : (si + 1) * e, ti * e : (ti + 1) * e] for j in range(4)
                )
                kpr, kpi, kmr, kmi = cc - ss, cs + sc, cc + ss, sc - cs
                rp = rp + (xpr * kpr - xpi * kpi)
                ip = ip + (xpi * kpr + xpr * kpi)
                rm = rm + (xmr * kmr + xmi * kmi)
                im = im + (xmi * kmr - xmr * kmi)
            upper += [rp + rm, -(ip + im)]
            lower += [im - ip, rm - rp]
        rows.append(
            jnp.concatenate([jnp.concatenate(upper, axis=1), jnp.concatenate(lower, axis=1)], axis=0)
        )
    p, m = (dot(back_left[si], stacked(rows[si])) for si in range(2))
    b2 = p[e:] - m[e:]
    b0 = SIGNS[0] * (p[:e] + m[:e]) + b2
    b1 = SIGNS[0] * (p[e:] + m[e:]) + (p[:e] - m[:e])
    back = jnp.concatenate([b0, b1, b2], axis=0)
    p, m = (
        dot(beside(back[:, ti * 2 * e : (ti + 1) * 2 * e]), back_right[ti]) for ti in range(2)
    )
    b2 = p[:, e:] - m[:, e:]
    b0 = SIGNS[0] * (p[:, :e] + m[:, :e]) + b2
    b1 = SIGNS[0] * (p[:, e:] + m[:, e:]) + (p[:, :e] - m[:, :e])
    result = jnp.concatenate([b0, b1, b2], axis=1) * inverse_rms[...] * scale
    scores[...] = result
    return jnp.max(result)


OUTSIDE = pl.BlockSpec(memory_space=pltpu.HBM)
INSIDE = pl.BlockSpec(memory_space=pltpu.VMEM)


def pick_call(block_owner, block_clips, layer_order, library, tiles, bits):
    _, layers, e, _ = library.shape
    blocks, per_block = block_clips.shape

    def kernel(owner_in, clips_in, order_in, library, tiles, *refs):
        mine, theirs, edge, owner_bits, order, owner, clips, layer, sems = refs
        small = [
            pltpu.make_async_copy(source, target, sems.at[i])
            for i, (source, target) in enumerate(
                ((clips_in, clips), (owner_in, owner), (order_in, layer))
            )
        ]
        for copy in small:
            copy.start()
        rows = [
            pltpu.make_async_copy(tiles.at[l, pl.ds(0, e), :], edge.at[l], sems.at[5 + l])
            for l in range(layers)
        ]
        for copy in rows:
            copy.start()
        me, block = lax.axis_index("tile"), lax.axis_index("groups") % 2
        core = me % 2
        small[0].wait()
        large = [
            pltpu.make_async_copy(library.at[clips[block, core]], mine, sems.at[3]),
            pltpu.make_async_copy(library.at[clips[block, 1 - core]], theirs, sems.at[4]),
        ]
        for copy in large:
            copy.start()
        small[1].wait()
        small[2].wait()
        differ = owner[block] ^ me
        row = lax.broadcasted_iota(jnp.int32, owner_bits.shape, 0)
        value = jnp.zeros(owner_bits.shape, jnp.int32)
        for k in range(bits):
            value = jnp.where(row == k, (differ >> k) & 1, value)
        owner_bits[...] = value
        value = jnp.zeros(owner_bits.shape, jnp.int32)
        for l in range(layers):
            value = jnp.where(row == l, layer[0, l], value)
        order[...] = value
        for copy in large + rows:
            copy.wait()

    clip = jax.ShapeDtypeStruct((layers, e, e), jnp.float32)
    edge = jax.ShapeDtypeStruct((layers, e, tiles.shape[-1]), jnp.float32)
    table = jax.ShapeDtypeStruct((8, e), jnp.int32)
    return pl.pallas_call(
        kernel,
        out_shape=(clip, clip, edge, table, table),
        in_specs=[OUTSIDE] * 5,
        out_specs=(INSIDE,) * 5,
        scratch_shapes=[
            pltpu.SMEM(block_owner.shape, jnp.int32),
            pltpu.SMEM(block_clips.shape, jnp.int32),
            pltpu.SMEM(layer_order.shape, jnp.int32),
            pltpu.SemaphoreType.DMA((5 + layers,)),
        ],
        compiler_params=pltpu.CompilerParams(vmem_limit_bytes=WHOLE),
    )(block_owner, block_clips, layer_order, library, tiles)


def tile_call(tiles, halo, own):
    layers, rows, columns = tiles.shape
    e = halo.shape[1]
    return pl.pallas_call(
        tile_kernel,
        in_specs=[INSIDE] * (2 + len(own)),
        out_specs=(INSIDE, INSIDE),
        out_shape=(
            jax.ShapeDtypeStruct((layers, 4, 2 * e, 2 * e), jnp.float32),
            jax.ShapeDtypeStruct((rows, columns), jnp.float32),
        ),
        compiler_params=pltpu.CompilerParams(vmem_limit_bytes=MOST),
        cost_estimate=pl.CostEstimate(flops=2_000_000_000, bytes_accessed=6_000_000, transcendentals=0),
    )(tiles, halo, *own)


def score_call(first, clips, order, spectrum, inverse_rms, consts, count, before):
    n = len(clips)
    layers, e, _ = clips[0].shape
    rows, columns = inverse_rms.shape
    args = (*clips, order, spectrum, inverse_rms, *consts)
    in_specs = [INSIDE] * len(args)
    aliases = {}
    if before is not None:
        in_specs.append(OUTSIDE)
        aliases = {len(args): 0}
        args += (before,)

    def kernel(*refs):
        scores, peaks, result, sems = refs[-4:]
        order, *rest = refs[n : n + 7]
        own = lax.axis_index("groups") % 2 * 2 + lax.axis_index("tile") % 2
        slots = [own ^ (first + i) for i in range(n)]
        row = lax.broadcasted_iota(jnp.int32, peaks.shape, 0)
        best = jnp.full(peaks.shape, -jnp.inf, jnp.float32)
        copies = []
        for i in range(n):
            if i > 1:
                copies[i - 2].wait()
            largest = score_clip(order, refs[i], *rest, result.at[i % 2])
            best = jnp.where(row == slots[i], largest, best)
            copies.append(pltpu.make_async_copy(result.at[i % 2], scores.at[slots[i]], sems.at[i % 2]))
            copies[i].start()
        peaks[...] = best
        for copy in copies[-2:]:
            copy.wait()

    return pl.pallas_call(
        kernel,
        in_specs=in_specs,
        out_specs=(OUTSIDE, INSIDE),
        out_shape=(
            jax.ShapeDtypeStruct((count, rows, columns), jnp.float32),
            jax.ShapeDtypeStruct((8, 128), jnp.float32),
        ),
        scratch_shapes=[
            pltpu.VMEM((2, rows, columns), jnp.float32),
            pltpu.SemaphoreType.DMA((2,)),
        ],
        input_output_aliases=aliases,
        compiler_params=pltpu.CompilerParams(vmem_limit_bytes=VMEM),
        cost_estimate=pl.CostEstimate(
            flops=n * 1_300_000_000, bytes_accessed=6_000_000, transcendentals=0
        ),
    )(*args)


def swap(block, axis, distance):
    return lax.ppermute(block, axis, [(i, i ^ distance) for i in range(lax.axis_size(axis))])


def cross_swap(block):
    groups, devices = lax.axis_size("groups"), lax.axis_size("tile")
    route = [
        (g * devices + i, (g ^ 1) * devices + (i ^ 1)) for g in range(groups) for i in range(devices)
    ]
    return lax.ppermute(block, ("groups", "tile"), route)


def local(tiles, library, block_owner, block_clips, layer_order):
    layers, rows, columns = tiles.shape
    e = library.shape[-1]
    assert rows == 3 * e and columns == 3 * e and layers * e <= 256
    blocks, per_block = block_clips.shape
    devices = lax.axis_size("tile")
    assert blocks == 2 and per_block == 2 and devices & (devices - 1) == 0
    tile_left, tile_right, clip_left, clip_right, back_left, back_right = map(jnp.asarray, factors(e))
    band_rows, band_cols = map(jnp.asarray, bands(e))

    bits = devices.bit_length() - 1
    mine, theirs, edge, differ, order = pick_call(
        block_owner, block_clips, layer_order, library, tiles, bits
    )
    own = (band_rows, band_cols, tile_right, tile_left)
    edge, tiles, own = lax.optimization_barrier((edge, tiles, own))
    halo = lax.ppermute(edge, "tile", [(i, i - 1) for i in range(1, devices)])

    def take(k, own, got):
        return jnp.where(differ[k][None, None, :] == 0, own, got)

    held = take(0, mine, swap(theirs, "tile", 1))
    consts = (clip_left, clip_right, back_left, back_right)
    for k in range(1, bits):
        got = swap(held, "tile", 1 << k)
        if k == 2:
            got, halo = lax.optimization_barrier((got, halo))
            spectrum, inverse_rms = tile_call(tiles, halo, own)
        held = take(k, held, got)
        if k == 3:
            held, spectrum, inverse_rms = lax.optimization_barrier((held, spectrum, inverse_rms))
    twin = swap(held, "tile", 1)
    other = swap(held, "groups", 1)
    cross = cross_swap(held)
    count = blocks * per_block
    shared = (order, spectrum, inverse_rms, consts, count)
    scores, best = score_call(0, (held, twin), *shared, None)
    scores, more = score_call(2, (other, cross), *shared, scores)
    best = jnp.maximum(best, more)
    distance = 1
    while distance < devices:
        best = jnp.maximum(best, swap(best, "tile", distance))
        distance *= 2
    return (
        scores.reshape(blocks, per_block, rows, columns),
        best[:count, 0].reshape(blocks, per_block),
    )


def solution(mesh):
    in_specs = (
        P(None, ("groups", "tile"), None),
        P("tile", None, None, None),
        P(),
        P(),
        P(("groups", "tile"), None),
    )
    out_specs = (P(None, None, ("groups", "tile"), None), P("groups", None))
    return jax.shard_map(local, mesh=mesh, in_specs=in_specs, out_specs=out_specs, check_vma=False)
```

```python
import math

import jax
import jax.numpy as jnp
import ml_dtypes
import numpy as np
from jax import lax
from jax.experimental import pallas as pl
from jax.experimental.pallas import tpu as pltpu
from jax.sharding import PartitionSpec as P

SIGNS = (math.sqrt(2.0), -math.sqrt(2.0))
VMEM = 20 * 1024 * 1024
MOST = 40 * 1024 * 1024
WHOLE = 8 * 1024 * 1024


def halves(matrix):
    high = matrix.astype(ml_dtypes.bfloat16)
    low = (matrix - high.astype(np.float64)).astype(ml_dtypes.bfloat16)
    return high, low


def evaluation(e, ring):
    k = np.arange(2 * e)
    k = k[np.isin(k % 4, (0, 3) if ring == 0 else (1, 2))]
    angles = np.outer(2 * k + 1, np.arange(2 * e)) % (8 * e) * (2.0 * np.pi / (8 * e))
    return np.concatenate([np.cos(angles), np.sin(angles)], axis=0)


def left_factor(matrix):
    high, low = halves(matrix)
    return np.concatenate([high, low, high], axis=1)


def right_factor(matrix):
    high, low = halves(matrix)
    return np.concatenate([high, low, high], axis=0)


def factors(e):
    ev = [evaluation(e, ring) for ring in range(2)]
    inv = [np.linalg.inv(m) / (4.0 * math.sqrt(2.0)) for m in ev]
    inv_cols = [np.linalg.inv(m) / (2.0 * math.sqrt(2.0)) for m in ev]
    tile_left = np.stack([left_factor(m) for m in ev])
    tile_right = np.stack([right_factor(m.T) for m in ev])
    clip_left = left_factor(np.concatenate([m[:, :e] for m in ev], axis=0))
    clip_right = right_factor(np.concatenate([m[:, :e].T for m in ev], axis=1))
    back_left = np.stack([left_factor(m) for m in inv])
    back_right = np.stack([right_factor(m.T) for m in inv_cols])
    return tile_left, tile_right, clip_left, clip_right, back_left, back_right


def bands(e):
    position = np.arange(2 * e)[None, :] - np.arange(e)[:, None]
    band = ((position >= 0) & (position < e)).astype(ml_dtypes.bfloat16)
    return np.concatenate([band, band], axis=1), np.concatenate([band.T, band.T], axis=0)


def split(values):
    high = values.astype(jnp.bfloat16)
    return high, (values - high.astype(jnp.float32)).astype(jnp.bfloat16)


def dot(a, b):
    return jnp.dot(a, b, preferred_element_type=jnp.float32)


def beside(values):
    high, low = split(values)
    return jnp.concatenate([high, high, low], axis=1)


def stacked(values):
    high, low = split(values)
    return jnp.concatenate([high, high, low], axis=0)


def tile_kernel(tile, halo, band_rows, band_cols, right, left, spectrum, inverse_rms):
    layers, rows, columns = tile.shape
    e = halo.shape[1]
    blocks = [[tile[l, b * e : (b + 1) * e, :] for b in range(3)] + [halo[l]] for l in range(layers)]
    squares = [sum(blocks[l][b] * blocks[l][b] for l in range(layers)) for b in range(4)]
    parts = [split(v) for v in squares]
    for b in range(3):
        tall = jnp.concatenate([parts[b][0], parts[b + 1][0], parts[b][1], parts[b + 1][1]], axis=0)
        summed = dot(band_rows[...], tall)
        high, low = split(summed)
        for c in range(3):
            pair = (high[:, c * e : (c + 2) * e], low[:, c * e : (c + 2) * e])
            if c < 2:
                energy = dot(jnp.concatenate(pair, axis=1), band_cols[...])
            else:
                energy = dot(pair[0], band_cols[:e, :]) + dot(pair[1], band_cols[:e, :])
            inverse_rms[b * e : (b + 1) * e, c * e : (c + 1) * e] = lax.rsqrt(
                energy * (1.0 / (layers * e * e)) + 1e-05
            )
    for l in range(layers):
        a0, a1, a2, a3 = blocks[l]
        for si, s in enumerate(SIGNS):
            folded = jnp.concatenate([a0 - a2 - s * a3, a1 + s * a2 + a3], axis=0)
            c0, c1, c2 = (folded[:, b * e : (b + 1) * e] for b in range(3))
            along = []
            for ti, t in enumerate(SIGNS):
                ring = jnp.concatenate([c0 - c2, c1 + t * c2], axis=1)
                along.append(dot(beside(ring), right[ti]))
            both = dot(left[si], stacked(jnp.concatenate(along, axis=1)))
            for ti in range(2):
                at = ti * 2 * e
                cc, cs = both[:e, at : at + e], both[:e, at + e : at + 2 * e]
                sc, ss = both[e:, at : at + e], both[e:, at + e : at + 2 * e]
                lanes = slice(ti * e, (ti + 1) * e)
                place = slice(si * e, (si + 1) * e)
                spectrum[l, 0, place, lanes] = cc - ss
                spectrum[l, 1, place, lanes] = -(cs + sc)
                spectrum[l, 2, place, lanes] = cc + ss
                spectrum[l, 3, place, lanes] = sc - cs


def score_clip(
    order, clip, spectrum, inverse_rms, clip_left, clip_right, back_left, back_right, scores
):
    layers, e, _ = clip.shape
    root = math.sqrt(layers * e * e)
    first = []
    for l in range(layers):
        matched = clip[0]
        for m in range(1, layers):
            matched = jnp.where(order[l : l + 1, :] == m, clip[m], matched)
        first.append(matched)
    total = sum(jnp.sum(v * v, keepdims=True) for v in first)
    scale = lax.rsqrt(total * (1.0 / (layers * e * e)) + 1e-05) * (1.0 / root)
    down = dot(clip_left[...], stacked(jnp.concatenate(first, axis=1)))
    both = [
        dot(beside(down[:, l * e : (l + 1) * e]), clip_right[...]) for l in range(layers)
    ]
    rows = []
    for si in range(2):
        upper, lower = [], []
        for ti in range(2):
            at, up = ti * 2 * e, si * 2 * e
            rp = ip = rm = im = 0.0
            for l in range(layers):
                cc, cs = both[l][up : up + e, at : at + e], both[l][up : up + e, at + e : at + 2 * e]
                sc = both[l][up + e : up + 2 * e, at : at + e]
                ss = both[l][up + e : up + 2 * e, at + e : at + 2 * e]
                xpr, xpi, xmr, xmi = (
                    spectrum[l, j, si * e : (si + 1) * e, ti * e : (ti + 1) * e] for j in range(4)
                )
                kpr, kpi, kmr, kmi = cc - ss, cs + sc, cc + ss, sc - cs
                rp = rp + (xpr * kpr - xpi * kpi)
                ip = ip + (xpi * kpr + xpr * kpi)
                rm = rm + (xmr * kmr + xmi * kmi)
                im = im + (xmi * kmr - xmr * kmi)
            upper += [rp + rm, -(ip + im)]
            lower += [im - ip, rm - rp]
        rows.append(
            jnp.concatenate([jnp.concatenate(upper, axis=1), jnp.concatenate(lower, axis=1)], axis=0)
        )
    p, m = (dot(back_left[si], stacked(rows[si])) for si in range(2))
    b2 = p[e:] - m[e:]
    b0 = SIGNS[0] * (p[:e] + m[:e]) + b2
    b1 = SIGNS[0] * (p[e:] + m[e:]) + (p[:e] - m[:e])
    back = jnp.concatenate([b0, b1, b2], axis=0)
    p, m = (
        dot(beside(back[:, ti * 2 * e : (ti + 1) * 2 * e]), back_right[ti]) for ti in range(2)
    )
    b2 = p[:, e:] - m[:, e:]
    b0 = SIGNS[0] * (p[:, :e] + m[:, :e]) + b2
    b1 = SIGNS[0] * (p[:, e:] + m[:, e:]) + (p[:, :e] - m[:, :e])
    result = jnp.concatenate([b0, b1, b2], axis=1) * inverse_rms[...] * scale
    scores[...] = result
    return jnp.max(result)


OUTSIDE = pl.BlockSpec(memory_space=pltpu.HBM)
INSIDE = pl.BlockSpec(memory_space=pltpu.VMEM)


def pick_call(block_owner, block_clips, layer_order, library, tiles, bits):
    _, layers, e, _ = library.shape
    blocks, per_block = block_clips.shape

    def kernel(owner_in, clips_in, order_in, library, tiles, *refs):
        mine, theirs, edge, owner_bits, order, owner, clips, layer, sems = refs
        small = [
            pltpu.make_async_copy(source, target, sems.at[i])
            for i, (source, target) in enumerate(
                ((clips_in, clips), (owner_in, owner), (order_in, layer))
            )
        ]
        for copy in small:
            copy.start()
        rows = [
            pltpu.make_async_copy(tiles.at[l, pl.ds(0, e), :], edge.at[l], sems.at[5 + l])
            for l in range(layers)
        ]
        for copy in rows:
            copy.start()
        me, block = lax.axis_index("tile"), lax.axis_index("groups") % 2
        core = me % 2
        small[0].wait()
        large = [
            pltpu.make_async_copy(library.at[clips[block, core]], mine, sems.at[3]),
            pltpu.make_async_copy(library.at[clips[block, 1 - core]], theirs, sems.at[4]),
        ]
        for copy in large:
            copy.start()
        small[1].wait()
        small[2].wait()
        differ = owner[block] ^ me
        row = lax.broadcasted_iota(jnp.int32, owner_bits.shape, 0)
        value = jnp.zeros(owner_bits.shape, jnp.int32)
        for k in range(bits):
            value = jnp.where(row == k, (differ >> k) & 1, value)
        owner_bits[...] = value
        value = jnp.zeros(owner_bits.shape, jnp.int32)
        for l in range(layers):
            value = jnp.where(row == l, layer[0, l], value)
        order[...] = value
        for copy in large + rows:
            copy.wait()

    clip = pltpu.VMEM((layers, e, e), jnp.float32)
    edge = pltpu.VMEM((layers, e, tiles.shape[-1]), jnp.float32)
    table = pltpu.VMEM((8, e), jnp.int32)
    args = (block_owner, block_clips, layer_order, library, tiles)
    args = [pltpu.with_memory_space_constraint(a, pltpu.HBM) for a in args]
    return pl.pallas_call(
        kernel,
        out_shape=(clip, clip, edge, table, table),
        in_specs=[OUTSIDE] * 5,
        out_specs=(INSIDE,) * 5,
        scratch_shapes=[
            pltpu.SMEM(block_owner.shape, jnp.int32),
            pltpu.SMEM(block_clips.shape, jnp.int32),
            pltpu.SMEM(layer_order.shape, jnp.int32),
            pltpu.SemaphoreType.DMA((5 + layers,)),
        ],
        compiler_params=pltpu.CompilerParams(vmem_limit_bytes=WHOLE),
    )(*args)


def hold_call(arrays):
    n = len(arrays)

    def kernel(*refs):
        copies = [
            pltpu.make_async_copy(refs[i], refs[n + i], refs[-1].at[i]) for i in range(n)
        ]
        for copy in copies:
            copy.start()
        for copy in copies:
            copy.wait()

    return pl.pallas_call(
        kernel,
        out_shape=tuple(pltpu.VMEM(a.shape, a.dtype) for a in arrays),
        in_specs=[OUTSIDE] * n,
        out_specs=(INSIDE,) * n,
        scratch_shapes=[pltpu.SemaphoreType.DMA((n,))],
        compiler_params=pltpu.CompilerParams(vmem_limit_bytes=WHOLE),
        cost_estimate=pl.CostEstimate(
            flops=0, bytes_accessed=2 * sum(a.nbytes for a in arrays), transcendentals=0
        ),
    )(*(pltpu.with_memory_space_constraint(a, pltpu.HBM) for a in arrays))


def tile_call(tiles, halo, own):
    layers, rows, columns = tiles.shape
    e = halo.shape[1]
    return pl.pallas_call(
        tile_kernel,
        in_specs=[INSIDE] * (2 + len(own)),
        out_specs=(INSIDE, INSIDE),
        out_shape=(
            jax.ShapeDtypeStruct((layers, 4, 2 * e, 2 * e), jnp.float32),
            jax.ShapeDtypeStruct((rows, columns), jnp.float32),
        ),
        compiler_params=pltpu.CompilerParams(vmem_limit_bytes=MOST),
        cost_estimate=pl.CostEstimate(flops=2_000_000_000, bytes_accessed=6_000_000, transcendentals=0),
    )(tiles, halo, *own)


def score_call(first, clips, order, spectrum, inverse_rms, consts, blocks, per_block):
    n = len(clips)
    rows, columns = inverse_rms.shape
    args = (*clips, order, spectrum, inverse_rms, *consts)

    def kernel(*refs):
        scores, peaks = refs[-2:]
        order, *rest = refs[n : n + 7]
        own = lax.axis_index("groups") % blocks * per_block + lax.axis_index("tile") % per_block
        row = lax.broadcasted_iota(jnp.int32, peaks.shape, 0)
        column = lax.broadcasted_iota(jnp.int32, peaks.shape, 1)
        best = jnp.full(peaks.shape, -jnp.inf, jnp.float32)
        for i in range(n):
            largest = score_clip(order, refs[i], *rest, scores.at[i])
            best = jnp.where(row * per_block + column == own ^ (first + i), largest, best)
        peaks[...] = best

    return pl.pallas_call(
        kernel,
        in_specs=[INSIDE] * len(args),
        out_specs=(INSIDE, INSIDE),
        out_shape=(
            pltpu.VMEM((n, rows, columns), jnp.float32),
            pltpu.VMEM((blocks, per_block), jnp.float32),
        ),
        compiler_params=pltpu.CompilerParams(vmem_limit_bytes=VMEM),
        cost_estimate=pl.CostEstimate(
            flops=n * 1_300_000_000, bytes_accessed=6_000_000, transcendentals=0
        ),
    )(*args)


def write_call(results, blocks, per_block):
    count = blocks * per_block
    rows, columns = results[0].shape[1:]

    def kernel(*refs):
        scores, sems = refs[-2:]
        own = lax.axis_index("groups") % blocks * per_block + lax.axis_index("tile") % per_block
        copies = []
        for ref in refs[:-2]:
            for i in range(ref.shape[0]):
                k = len(copies)
                copies.append(pltpu.make_async_copy(ref.at[i], scores.at[own ^ k], sems.at[k]))
                copies[k].start()
        for copy in copies:
            copy.wait()

    return pl.pallas_call(
        kernel,
        in_specs=[INSIDE] * len(results),
        out_specs=OUTSIDE,
        out_shape=jax.ShapeDtypeStruct((count, rows, columns), jnp.float32),
        scratch_shapes=[pltpu.SemaphoreType.DMA((count,))],
        compiler_params=pltpu.CompilerParams(vmem_limit_bytes=WHOLE),
        cost_estimate=pl.CostEstimate(
            flops=0, bytes_accessed=2 * count * rows * columns * 4, transcendentals=0
        ),
    )(*results)


def swap(block, axis, distance):
    return lax.ppermute(block, axis, [(i, i ^ distance) for i in range(lax.axis_size(axis))])


def local(tiles, library, block_owner, block_clips, layer_order):
    layers, rows, columns = tiles.shape
    e = library.shape[-1]
    assert rows == 3 * e and columns == 3 * e and layers * e <= 256
    blocks, per_block = block_clips.shape
    devices = lax.axis_size("tile")
    assert blocks == 2 and per_block == 2 and devices & (devices - 1) == 0
    tile_left, tile_right, clip_left, clip_right, back_left, back_right = map(jnp.asarray, factors(e))
    band_rows, band_cols = map(jnp.asarray, bands(e))

    bits = devices.bit_length() - 1
    mine, theirs, edge, differ, order = pick_call(
        block_owner, block_clips, layer_order, library, tiles, bits
    )
    halo = lax.ppermute(edge, "tile", [(i, i - 1) for i in range(1, devices)])

    def take(k, own, got):
        return jnp.where(differ[k][None, None, :] == 0, own, got)

    held = take(0, mine, swap(theirs, "tile", 1))
    own = (tiles, band_rows, band_cols, tile_right, tile_left)
    held, own = lax.optimization_barrier((held, own))
    tiles, *own = hold_call(own)
    consts = (clip_left, clip_right, back_left, back_right)
    for k in range(1, bits):
        got = swap(held, "tile", 1 << k)
        if k == 2:
            got, halo = lax.optimization_barrier((got, halo))
            spectrum, inverse_rms = tile_call(tiles, halo, own)
        held = take(k, held, got)
        if k == 3:
            held, spectrum, inverse_rms = lax.optimization_barrier((held, spectrum, inverse_rms))
    twin = swap(held, "tile", 1)
    other = swap(held, "groups", 1)
    shared = (order, spectrum, inverse_rms, consts, blocks, per_block)
    near, best = score_call(0, (held, twin), *shared)
    other, near = lax.optimization_barrier((other, near))
    cross = swap(other, "tile", 1)
    far, more = score_call(2, (other,), *shared)
    best = jnp.maximum(best, more)
    cross, far = lax.optimization_barrier((cross, far))
    last, more = score_call(3, (cross,), *shared)
    best = jnp.maximum(best, more)
    best = jnp.maximum(best, swap(best, "tile", 1))
    best, near, far, last = lax.optimization_barrier((best, near, far, last))
    scores = write_call((near, far, last), blocks, per_block)
    for k in range(1, bits):
        got = swap(best, "tile", 1 << k)
        if k == 2:
            got, scores = lax.optimization_barrier((got, scores))
        best = jnp.maximum(best, got)
    return scores.reshape(blocks, per_block, rows, columns), best


def solution(mesh):
    in_specs = (
        P(None, ("groups", "tile"), None),
        P("tile", None, None, None),
        P(),
        P(),
        P(("groups", "tile"), None),
    )
    out_specs = (P(None, None, ("groups", "tile"), None), P("groups", None))
    return jax.shard_map(local, mesh=mesh, in_specs=in_specs, out_specs=out_specs, check_vma=False)
```

```python
import math

import jax
import jax.numpy as jnp
import ml_dtypes
import numpy as np
from jax import lax
from jax.experimental import pallas as pl
from jax.experimental.pallas import tpu as pltpu
from jax.sharding import PartitionSpec as P

SIGNS = (math.sqrt(2.0), -math.sqrt(2.0))
VMEM = 20 * 1024 * 1024
MOST = 40 * 1024 * 1024
WHOLE = 8 * 1024 * 1024


def halves(matrix):
    high = matrix.astype(ml_dtypes.bfloat16)
    low = (matrix - high.astype(np.float64)).astype(ml_dtypes.bfloat16)
    return high, low


def evaluation(e, ring):
    k = np.arange(2 * e)
    k = k[np.isin(k % 4, (0, 3) if ring == 0 else (1, 2))]
    angles = np.outer(2 * k + 1, np.arange(2 * e)) % (8 * e) * (2.0 * np.pi / (8 * e))
    return np.concatenate([np.cos(angles), np.sin(angles)], axis=0)


def left_factor(matrix):
    high, low = halves(matrix)
    return np.concatenate([high, low, high], axis=1)


def right_factor(matrix):
    high, low = halves(matrix)
    return np.concatenate([high, low, high], axis=0)


def factors(e):
    ev = [evaluation(e, ring) for ring in range(2)]
    inv = [np.linalg.inv(m) / (4.0 * math.sqrt(2.0)) for m in ev]
    inv_cols = [np.linalg.inv(m) / (2.0 * math.sqrt(2.0)) for m in ev]
    tile_left = np.stack([left_factor(m) for m in ev])
    tile_right = np.stack([right_factor(m.T) for m in ev])
    clip_left = left_factor(np.concatenate([m[:, :e] for m in ev], axis=0))
    clip_right = right_factor(np.concatenate([m[:, :e].T for m in ev], axis=1))
    back_left = np.stack([left_factor(m) for m in inv])
    back_right = np.stack([right_factor(m.T) for m in inv_cols])
    return tile_left, tile_right, clip_left, clip_right, back_left, back_right


def bands(e):
    position = np.arange(2 * e)[None, :] - np.arange(e)[:, None]
    band = ((position >= 0) & (position < e)).astype(ml_dtypes.bfloat16)
    return np.concatenate([band, band], axis=1), np.concatenate([band.T, band.T], axis=0)


def split(values):
    high = values.astype(jnp.bfloat16)
    return high, (values - high.astype(jnp.float32)).astype(jnp.bfloat16)


def dot(a, b):
    return jnp.dot(a, b, preferred_element_type=jnp.float32)


def beside(values):
    high, low = split(values)
    return jnp.concatenate([high, high, low], axis=1)


def stacked(values):
    high, low = split(values)
    return jnp.concatenate([high, high, low], axis=0)


def tile_kernel(tile, halo, band_rows, band_cols, right, left, spectrum, inverse_rms):
    layers, rows, columns = tile.shape
    e = halo.shape[1]
    blocks = [[tile[l, b * e : (b + 1) * e, :] for b in range(3)] + [halo[l]] for l in range(layers)]
    squares = [sum(blocks[l][b] * blocks[l][b] for l in range(layers)) for b in range(4)]
    parts = [split(v) for v in squares]
    for b in range(3):
        tall = jnp.concatenate([parts[b][0], parts[b + 1][0], parts[b][1], parts[b + 1][1]], axis=0)
        summed = dot(band_rows[...], tall)
        high, low = split(summed)
        for c in range(3):
            pair = (high[:, c * e : (c + 2) * e], low[:, c * e : (c + 2) * e])
            if c < 2:
                energy = dot(jnp.concatenate(pair, axis=1), band_cols[...])
            else:
                energy = dot(pair[0], band_cols[:e, :]) + dot(pair[1], band_cols[:e, :])
            inverse_rms[b * e : (b + 1) * e, c * e : (c + 1) * e] = lax.rsqrt(
                energy * (1.0 / (layers * e * e)) + 1e-05
            )
    for l in range(layers):
        a0, a1, a2, a3 = blocks[l]
        for si, s in enumerate(SIGNS):
            folded = jnp.concatenate([a0 - a2 - s * a3, a1 + s * a2 + a3], axis=0)
            c0, c1, c2 = (folded[:, b * e : (b + 1) * e] for b in range(3))
            along = []
            for ti, t in enumerate(SIGNS):
                ring = jnp.concatenate([c0 - c2, c1 + t * c2], axis=1)
                along.append(dot(beside(ring), right[ti]))
            both = dot(left[si], stacked(jnp.concatenate(along, axis=1)))
            for ti in range(2):
                at = ti * 2 * e
                cc, cs = both[:e, at : at + e], both[:e, at + e : at + 2 * e]
                sc, ss = both[e:, at : at + e], both[e:, at + e : at + 2 * e]
                lanes = slice(ti * e, (ti + 1) * e)
                place = slice(si * e, (si + 1) * e)
                spectrum[l, 0, place, lanes] = cc - ss
                spectrum[l, 1, place, lanes] = -(cs + sc)
                spectrum[l, 2, place, lanes] = cc + ss
                spectrum[l, 3, place, lanes] = sc - cs


def score_clip(
    order, clip, spectrum, inverse_rms, clip_left, clip_right, back_left, back_right, scores
):
    layers, e, _ = clip.shape
    root = math.sqrt(layers * e * e)
    first = []
    for l in range(layers):
        matched = clip[0]
        for m in range(1, layers):
            matched = jnp.where(order[l : l + 1, :] == m, clip[m], matched)
        first.append(matched)
    total = sum(jnp.sum(v * v, keepdims=True) for v in first)
    scale = lax.rsqrt(total * (1.0 / (layers * e * e)) + 1e-05) * (1.0 / root)
    down = dot(clip_left[...], stacked(jnp.concatenate(first, axis=1)))
    both = [
        dot(beside(down[:, l * e : (l + 1) * e]), clip_right[...]) for l in range(layers)
    ]
    rows = []
    for si in range(2):
        upper, lower = [], []
        for ti in range(2):
            at, up = ti * 2 * e, si * 2 * e
            rp = ip = rm = im = 0.0
            for l in range(layers):
                cc, cs = both[l][up : up + e, at : at + e], both[l][up : up + e, at + e : at + 2 * e]
                sc = both[l][up + e : up + 2 * e, at : at + e]
                ss = both[l][up + e : up + 2 * e, at + e : at + 2 * e]
                xpr, xpi, xmr, xmi = (
                    spectrum[l, j, si * e : (si + 1) * e, ti * e : (ti + 1) * e] for j in range(4)
                )
                kpr, kpi, kmr, kmi = cc - ss, cs + sc, cc + ss, sc - cs
                rp = rp + (xpr * kpr - xpi * kpi)
                ip = ip + (xpi * kpr + xpr * kpi)
                rm = rm + (xmr * kmr + xmi * kmi)
                im = im + (xmi * kmr - xmr * kmi)
            upper += [rp + rm, -(ip + im)]
            lower += [im - ip, rm - rp]
        rows.append(
            jnp.concatenate([jnp.concatenate(upper, axis=1), jnp.concatenate(lower, axis=1)], axis=0)
        )
    p, m = (dot(back_left[si], stacked(rows[si])) for si in range(2))
    b2 = p[e:] - m[e:]
    b0 = SIGNS[0] * (p[:e] + m[:e]) + b2
    b1 = SIGNS[0] * (p[e:] + m[e:]) + (p[:e] - m[:e])
    back = jnp.concatenate([b0, b1, b2], axis=0)
    p, m = (
        dot(beside(back[:, ti * 2 * e : (ti + 1) * 2 * e]), back_right[ti]) for ti in range(2)
    )
    b2 = p[:, e:] - m[:, e:]
    b0 = SIGNS[0] * (p[:, :e] + m[:, :e]) + b2
    b1 = SIGNS[0] * (p[:, e:] + m[:, e:]) + (p[:, :e] - m[:, :e])
    result = jnp.concatenate([b0, b1, b2], axis=1) * inverse_rms[...] * scale
    scores[...] = result
    return jnp.max(result)


OUTSIDE = pl.BlockSpec(memory_space=pltpu.HBM)
INSIDE = pl.BlockSpec(memory_space=pltpu.VMEM)


def pick_call(block_owner, block_clips, layer_order, library, tiles, bits):
    _, layers, e, _ = library.shape
    blocks, per_block = block_clips.shape

    def kernel(owner_in, clips_in, order_in, library, tiles, *refs):
        mine, theirs, edge, owner_bits, order, owner, clips, layer, sems = refs
        small = [
            pltpu.make_async_copy(source, target, sems.at[i])
            for i, (source, target) in enumerate(
                ((clips_in, clips), (owner_in, owner), (order_in, layer))
            )
        ]
        for copy in small:
            copy.start()
        rows = [
            pltpu.make_async_copy(tiles.at[l, pl.ds(0, e), :], edge.at[l], sems.at[5 + l])
            for l in range(layers)
        ]
        for copy in rows:
            copy.start()
        me, block = lax.axis_index("tile"), lax.axis_index("groups") % 2
        core = me % 2
        small[0].wait()
        large = [
            pltpu.make_async_copy(library.at[clips[block, core]], mine, sems.at[3]),
            pltpu.make_async_copy(library.at[clips[block, 1 - core]], theirs, sems.at[4]),
        ]
        for copy in large:
            copy.start()
        small[1].wait()
        small[2].wait()
        differ = owner[block] ^ me
        row = lax.broadcasted_iota(jnp.int32, owner_bits.shape, 0)
        value = jnp.zeros(owner_bits.shape, jnp.int32)
        for k in range(bits):
            value = jnp.where(row == k, (differ >> k) & 1, value)
        owner_bits[...] = value
        value = jnp.zeros(owner_bits.shape, jnp.int32)
        for l in range(layers):
            value = jnp.where(row == l, layer[0, l], value)
        order[...] = value
        for copy in large + rows:
            copy.wait()

    clip = pltpu.VMEM((layers, e, e), jnp.float32)
    edge = pltpu.VMEM((layers, e, tiles.shape[-1]), jnp.float32)
    table = pltpu.VMEM((8, e), jnp.int32)
    args = (block_owner, block_clips, layer_order, library, tiles)
    args = [pltpu.with_memory_space_constraint(a, pltpu.HBM) for a in args]
    return pl.pallas_call(
        kernel,
        out_shape=(clip, clip, edge, table, table),
        in_specs=[OUTSIDE] * 5,
        out_specs=(INSIDE,) * 5,
        scratch_shapes=[
            pltpu.SMEM(block_owner.shape, jnp.int32),
            pltpu.SMEM(block_clips.shape, jnp.int32),
            pltpu.SMEM(layer_order.shape, jnp.int32),
            pltpu.SemaphoreType.DMA((5 + layers,)),
        ],
        compiler_params=pltpu.CompilerParams(vmem_limit_bytes=WHOLE),
    )(*args)


def hold_call(arrays):
    n = len(arrays)

    def kernel(*refs):
        copies = [
            pltpu.make_async_copy(refs[i], refs[n + i], refs[-1].at[i]) for i in range(n)
        ]
        for copy in copies:
            copy.start()
        for copy in copies:
            copy.wait()

    return pl.pallas_call(
        kernel,
        out_shape=tuple(pltpu.VMEM(a.shape, a.dtype) for a in arrays),
        in_specs=[OUTSIDE] * n,
        out_specs=(INSIDE,) * n,
        scratch_shapes=[pltpu.SemaphoreType.DMA((n,))],
        compiler_params=pltpu.CompilerParams(vmem_limit_bytes=WHOLE),
        cost_estimate=pl.CostEstimate(
            flops=0, bytes_accessed=2 * sum(a.nbytes for a in arrays), transcendentals=0
        ),
    )(*(pltpu.with_memory_space_constraint(a, pltpu.HBM) for a in arrays))


def tile_call(tiles, halo, own):
    layers, rows, columns = tiles.shape
    e = halo.shape[1]
    return pl.pallas_call(
        tile_kernel,
        in_specs=[INSIDE] * (2 + len(own)),
        out_specs=(INSIDE, INSIDE),
        out_shape=(
            jax.ShapeDtypeStruct((layers, 4, 2 * e, 2 * e), jnp.float32),
            jax.ShapeDtypeStruct((rows, columns), jnp.float32),
        ),
        compiler_params=pltpu.CompilerParams(vmem_limit_bytes=MOST),
        cost_estimate=pl.CostEstimate(flops=2_000_000_000, bytes_accessed=6_000_000, transcendentals=0),
    )(tiles, halo, *own)


def score_call(first, clips, order, spectrum, inverse_rms, consts, blocks, per_block):
    n = len(clips)
    rows, columns = inverse_rms.shape
    args = (*clips, order, spectrum, inverse_rms, *consts)

    def kernel(*refs):
        scores, peaks = refs[-2:]
        order, *rest = refs[n : n + 7]
        own = lax.axis_index("groups") % blocks * per_block + lax.axis_index("tile") % per_block
        row = lax.broadcasted_iota(jnp.int32, peaks.shape, 0)
        column = lax.broadcasted_iota(jnp.int32, peaks.shape, 1)
        best = jnp.full(peaks.shape, -jnp.inf, jnp.float32)
        for i in range(n):
            largest = score_clip(order, refs[i], *rest, scores.at[i])
            best = jnp.where(row * per_block + column == own ^ (first + i), largest, best)
        peaks[...] = best

    return pl.pallas_call(
        kernel,
        in_specs=[INSIDE] * len(args),
        out_specs=(INSIDE, INSIDE),
        out_shape=(
            pltpu.VMEM((n, rows, columns), jnp.float32),
            pltpu.VMEM((blocks, per_block), jnp.float32),
        ),
        compiler_params=pltpu.CompilerParams(vmem_limit_bytes=VMEM),
        cost_estimate=pl.CostEstimate(
            flops=n * 1_300_000_000, bytes_accessed=6_000_000, transcendentals=0
        ),
    )(*args)


def write_call(results, blocks, per_block):
    count = blocks * per_block
    rows, columns = results[0].shape[1:]

    def kernel(*refs):
        scores, sems = refs[-2:]
        own = lax.axis_index("groups") % blocks * per_block + lax.axis_index("tile") % per_block
        copies = []
        for ref in refs[:-2]:
            for i in range(ref.shape[0]):
                k = len(copies)
                copies.append(pltpu.make_async_copy(ref.at[i], scores.at[own ^ k], sems.at[k]))
                copies[k].start()
        for copy in copies:
            copy.wait()

    return pl.pallas_call(
        kernel,
        in_specs=[INSIDE] * len(results),
        out_specs=OUTSIDE,
        out_shape=jax.ShapeDtypeStruct((count, rows, columns), jnp.float32),
        scratch_shapes=[pltpu.SemaphoreType.DMA((count,))],
        compiler_params=pltpu.CompilerParams(vmem_limit_bytes=WHOLE),
        cost_estimate=pl.CostEstimate(
            flops=0, bytes_accessed=2 * count * rows * columns * 4, transcendentals=0
        ),
    )(*results)


def swap(block, axis, distance):
    return lax.ppermute(block, axis, [(i, i ^ distance) for i in range(lax.axis_size(axis))])


def local(tiles, library, block_owner, block_clips, layer_order):
    layers, rows, columns = tiles.shape
    e = library.shape[-1]
    assert rows == 3 * e and columns == 3 * e and layers * e <= 256
    blocks, per_block = block_clips.shape
    devices = lax.axis_size("tile")
    assert blocks == 2 and per_block == 2 and devices & (devices - 1) == 0
    tile_left, tile_right, clip_left, clip_right, back_left, back_right = map(jnp.asarray, factors(e))
    band_rows, band_cols = map(jnp.asarray, bands(e))

    bits = devices.bit_length() - 1
    mine, theirs, edge, differ, order = pick_call(
        block_owner, block_clips, layer_order, library, tiles, bits
    )
    halo = lax.ppermute(edge, "tile", [(i, i - 1) for i in range(1, devices)])

    def take(k, own, got):
        return jnp.where(differ[k][None, None, :] == 0, own, got)

    held = take(0, mine, swap(theirs, "tile", 1))
    own = (tiles, band_rows, band_cols, tile_right, tile_left)
    held, own = lax.optimization_barrier((held, own))
    tiles, *own = hold_call(own)
    consts = (clip_left, clip_right, back_left, back_right)
    for k in range(1, bits):
        got = swap(held, "tile", 1 << k)
        if k == 2:
            got, halo = lax.optimization_barrier((got, halo))
            spectrum, inverse_rms = tile_call(tiles, halo, own)
        held = take(k, held, got)
        if k == 3:
            held, spectrum, inverse_rms = lax.optimization_barrier((held, spectrum, inverse_rms))
    twin = swap(held, "tile", 1)
    other = swap(held, "groups", 1)
    shared = (order, spectrum, inverse_rms, consts, blocks, per_block)
    near, best = score_call(0, (held, twin), *shared)
    other, near = lax.optimization_barrier((other, near))
    cross = swap(other, "tile", 1)
    far, more = score_call(2, (other,), *shared)
    best = jnp.maximum(best, more)
    cross, far = lax.optimization_barrier((cross, far))
    last, more = score_call(3, (cross,), *shared)
    best = jnp.maximum(best, more)
    tail = [*range(1, bits), 0]
    best = jnp.maximum(best, swap(best, "tile", 1 << tail[0]))
    best, near, far, last = lax.optimization_barrier((best, near, far, last))
    scores = write_call((near, far, last), blocks, per_block)
    for step, k in enumerate(tail[1:], 1):
        got = swap(best, "tile", 1 << k)
        if step == 2:
            got, scores = lax.optimization_barrier((got, scores))
        best = jnp.maximum(best, got)
    return scores.reshape(blocks, per_block, rows, columns), best


def solution(mesh):
    in_specs = (
        P(None, ("groups", "tile"), None),
        P("tile", None, None, None),
        P(),
        P(),
        P(("groups", "tile"), None),
    )
    out_specs = (P(None, None, ("groups", "tile"), None), P("groups", None))
    return jax.shard_map(local, mesh=mesh, in_specs=in_specs, out_specs=out_specs, check_vma=False)
```
